32 devices in a mesh: store: 8 (over z, core), own: 4 (over y, x).
Axes of the slice: x: 2, y: 2, z: 4, core: 2. Of those that a mesh axis runs over, the one named last changes fastest.
Arguments:
- embed: bfloat16 [8192, 768], P(('store', 'own')), may hold values from -16 to 16
- cluster: int32 [8192], P(('store', 'own')), may hold values from 0 to 511, as said below
- rank: int32 [8192], P(('store', 'own')), may hold values from 0 to 8191, each once
Outputs:
- best_similarity: float32 [8192], P(('store', 'own'))
The draws below stay inside these ranges and needn't reach their ends.
Inputs may be any that keep to these rules, and one draw needn't show every extreme that they name: Among the 256 rows of one device, at most 33 have clusters with one owner (cluster mod 8); every device reaches 33 for some owners, and some owner gets exactly 33 from every device. `rank`: every value appears once.
All inputs are finite; a program needn't handle non-finite values.
Results may differ from the reference program's by a relative error of at most 0.00064.
Values may be sent and summed in bfloat16 or wider, within the bound.
No kernel may reach another device: no remote copies, remote signals or barrier semaphores. Data moves between devices by JAX's collectives and lax.ppermute only.
A program may use at most 64 MiB of HBM per device.

```python
import jax
import jax.numpy as jnp
from jax import lax

D = 768
CLUSTERS = 512
ROW_DEV = 256
CPO = 64
ROWS = 8192
N_STORE = 8


def cluster_ids(key):
    base = jax.random.fold_in(key, 101)
    pick_order = jax.random.permutation(jax.random.fold_in(base, 1), CPO).astype(jnp.int32)
    full_owner = jax.random.randint(jax.random.fold_in(base, 2), (), 0, N_STORE).astype(jnp.int32)
    per_owner = ROW_DEV // N_STORE
    block_keys = jax.random.split(jax.random.fold_in(base, 3), ROWS // ROW_DEV)

    def one_block(block_key):
        key_order = jax.random.fold_in(block_key, 1)
        key_spread = jax.random.fold_in(block_key, 2)
        key_first = jax.random.fold_in(block_key, 3)
        key_pick = jax.random.fold_in(block_key, 4)
        owner_order = jax.random.permutation(key_order, N_STORE).astype(jnp.int32)
        located = jnp.argmax(owner_order == full_owner)
        owner_order = owner_order.at[located].set(owner_order[0]).at[0].set(full_owner)
        ranked_counts = jnp.where(jnp.arange(N_STORE) < N_STORE // 2, per_owner + 1, per_owner - 1).astype(jnp.int32)
        counts = jnp.zeros((N_STORE,), jnp.int32).at[owner_order].set(ranked_counts)
        target = jnp.repeat(jnp.arange(N_STORE, dtype=jnp.int32), counts, total_repeat_length=ROW_DEV)
        target = jax.random.permutation(key_spread, target)
        upper = jax.random.randint(key_first, (ROW_DEV,), 0, CPO)
        chosen = jax.random.randint(key_pick, (ROW_DEV,), 0, 1 << 20) % (upper + 1)
        return target + N_STORE * pick_order[chosen]
    return jax.vmap(one_block)(block_keys).reshape(ROWS).astype(jnp.int32)


def draw_cluster(key, part):
    shared = cluster_ids(key)
    return shared


def draw_embed(key, part):
    shared = cluster_ids(key)
    key = jax.random.fold_in(key, 7)
    key_centre = jax.random.fold_in(key, 1)
    key_twin = jax.random.fold_in(key, 2)
    key_group = jax.random.fold_in(key, 3)
    key_noise = jax.random.fold_in(key, 4)
    centres = jax.random.normal(key_centre, (CLUSTERS, D), jnp.float32)
    twins = jax.random.normal(key_twin, (CLUSTERS * 16, D), jnp.float32)
    group = jax.random.randint(key_group, (ROWS,), 0, 16)
    noise = jax.random.normal(key_noise, (ROWS, D), jnp.float32)
    scales = jnp.ones((ROWS, 1), jnp.float32)
    values = 0.5 * centres[shared] + 0.7 * twins[shared * 16 + group] + 0.5 * noise
    return jnp.clip(values * scales, -16.0, 16.0).astype(jnp.bfloat16)


def setup_inputs(seed: int = 0) -> dict:
    seeds = jax.random.split(jax.random.key(seed), 4)
    embed = draw_embed(jax.random.fold_in(seeds[3], 71), 0)
    cluster = draw_cluster(jax.random.fold_in(seeds[3], 71), 0)
    rank = jax.random.permutation(seeds[2], ROWS).astype(jnp.int32)
    return {"embed": embed, "cluster": cluster, "rank": rank}


tile_rows = 512

def reference(embed, cluster, rank):
    widened = embed.astype(jnp.float32)
    unit_rows = (widened * lax.rsqrt(lax.optimization_barrier(jnp.sum(widened * widened, axis=1, keepdims=True)) + 1e-06)).astype(jnp.bfloat16)
    sort_key = cluster * ROWS + rank
    sort_order = jnp.argsort(sort_key).astype(jnp.int32)
    sorted_unit = unit_rows[sort_order]
    sorted_cluster = cluster[sort_order]
    sorted_rank = rank[sort_order]
    cluster_start = jnp.searchsorted(sorted_cluster, sorted_cluster, side='left').astype(jnp.int32)

    def one_block(block_index):
        offset = (block_index * tile_rows).astype(jnp.int32)
        query_rows = lax.dynamic_slice_in_dim(sorted_unit, offset, tile_rows)
        query_cluster = lax.dynamic_slice_in_dim(sorted_cluster, offset, tile_rows)
        query_rank = lax.dynamic_slice_in_dim(sorted_rank, offset, tile_rows)
        first_block = (lax.dynamic_index_in_dim(cluster_start, offset, keepdims=False) // tile_rows).astype(jnp.int32)

        def step(key_block, best_match):
            key_offset = (key_block * tile_rows).astype(jnp.int32)
            key_rows = lax.dynamic_slice_in_dim(sorted_unit, key_offset, tile_rows)
            key_cluster = lax.dynamic_slice_in_dim(sorted_cluster, key_offset, tile_rows)
            key_rank = lax.dynamic_slice_in_dim(sorted_rank, key_offset, tile_rows)
            scores = jnp.dot(query_rows, key_rows.T, preferred_element_type=jnp.float32)
            usable = (query_cluster[:, None] == key_cluster[None, :]) & (key_rank[None, :] < query_rank[:, None])
            return jnp.maximum(best_match, lax.optimization_barrier(jnp.max(jnp.where(usable, scores, -1.0), axis=1)))
        start_best = jnp.full((tile_rows,), -1.0, jnp.float32)
        return lax.fori_loop(first_block, (block_index + 1).astype(jnp.int32), step, start_best)
    blocks = lax.map(one_block, jnp.arange(ROWS // tile_rows, dtype=jnp.int32))
    return jnp.zeros((ROWS,), jnp.float32).at[sort_order].set(blocks.reshape(ROWS))
```

```python
import functools
from typing import NamedTuple

import jax
import jax.numpy as jnp
from jax import lax
from jax.experimental import pallas as pl
from jax.experimental.pallas import tpu as pltpu
from jax.sharding import Mesh, PartitionSpec as P

LANES = 128
TAIL = 16
CLUSTER_DIGITS = 2
RANK_DIGITS = 3
VMEM_LIMIT = 48 * 1024 * 1024


class Shape(NamedTuple):
    rows: int
    width: int
    z: int
    x: int
    y: int

    @property
    def classes(self):
        return self.z * self.x

    @property
    def capacity(self):
        return self.rows // self.classes + 1

    @property
    def base(self):
        return max(16, (self.rows // self.classes) // 16 * 16)

    @property
    def extra(self):
        return max(0, self.capacity - self.base)

    @property
    def stride(self):
        return self.base + 8 * self.extra

    @property
    def chunks(self):
        return self.width // LANES

    @property
    def tail_at(self):
        return self.chunks * self.base

    @property
    def block_rows(self):
        return self.tail_at + TAIL

    @property
    def per_lane_tile(self):
        return LANES // self.base

    @property
    def query_rows(self):
        return self.classes * self.base + (-(-self.classes // 16) * 16 if self.extra else 0)


def iota(shape, dim):
    return lax.broadcasted_iota(jnp.int32, shape, dim)


def my_class(s):
    return lax.axis_index("z") * s.x + lax.axis_index("x")


def row_of(ref):
    return jnp.concatenate([ref[i : i + 1, :] for i in range(ref.shape[0])], axis=1)


def dot(left, right, contract=((1,), (0,))):
    return lax.dot_general(left, right, (contract, ((), ())), preferred_element_type=jnp.float32)


def place_kernel(s, layout, embed_ref, cluster_ref, rank_ref, info_ref, *out_refs):
    widened = embed_ref[...].astype(jnp.float32)
    total = jnp.sum(widened * widened, axis=1, keepdims=True)
    unit = (widened * lax.rsqrt(total + 1e-06)).astype(jnp.bfloat16)
    cluster = row_of(cluster_ref)
    rank = row_of(rank_ref)
    n = s.classes
    shift = n.bit_length() - 1
    target = cluster & (n - 1)
    relative = target ^ my_class(s)
    member = (iota((n, s.rows), 0) == relative).astype(jnp.float32)
    earlier = (iota((s.rows, s.rows), 0) < iota((s.rows, s.rows), 1)).astype(jnp.float32)
    before = dot(member.astype(jnp.bfloat16), earlier.astype(jnp.bfloat16))
    within = jnp.sum(before * member, axis=0, keepdims=True).astype(jnp.int32)
    position = relative * s.stride + within
    placed = (iota((n * s.stride, s.rows), 0) == position).astype(jnp.float32).astype(jnp.bfloat16)
    grouped = dot(placed, unit)
    local = (cluster >> shift) + 1
    digits = [(local >> (8 * i)) & 255 for i in range(CLUSTER_DIGITS)]
    digits += [(rank >> (8 * i)) & 255 for i in range(RANK_DIGITS)]
    line = iota((TAIL, s.rows), 0)
    fields = jnp.zeros((TAIL, s.rows), jnp.int32)
    for i, digit in enumerate(digits):
        fields = jnp.where(line == s.chunks + i, digit, fields)
    spread = dot(fields.astype(jnp.float32).astype(jnp.bfloat16), placed, ((1,), (1,)))
    tail_line = iota((TAIL, LANES), 0)
    for ref, members in zip(out_refs, layout):
        for slot, r in enumerate(members):
            at = r * s.stride
            for c in range(s.chunks):
                ref[slot, c * s.base : (c + 1) * s.base, :] = grouped[
                    at : at + s.base, c * LANES : (c + 1) * LANES
                ].astype(jnp.bfloat16)
            tail = jnp.concatenate(
                [spread[:, at : at + s.stride], jnp.zeros((TAIL, LANES - s.stride), jnp.float32)], axis=1
            )
            if s.extra:
                for c in range(s.chunks):
                    piece = grouped[at + s.base : at + s.base + 1, c * LANES : (c + 1) * LANES]
                    tail = jnp.where(tail_line == c, piece, tail)
            ref[slot, s.tail_at : s.block_rows, :] = tail.astype(jnp.bfloat16)
    info_ref[...] = jnp.concatenate([target, within], axis=0)


def place(s, layout, embed, cluster, rank):
    outs = [jax.ShapeDtypeStruct((2, s.rows), jnp.int32)]
    outs += [jax.ShapeDtypeStruct((len(m), s.block_rows, LANES), jnp.bfloat16) for m in layout]
    return pl.pallas_call(
        functools.partial(place_kernel, s, layout),
        out_shape=outs,
        compiler_params=pltpu.CompilerParams(vmem_limit_bytes=VMEM_LIMIT),
        name="place",
    )(embed, cluster.reshape(-1, LANES), rank.reshape(-1, LANES))


def blocks_of(refs):
    return [(ref, j) for ref in refs for j in range(ref.shape[0])]


def unpack(s, blocks, rows_ref, tail_ref):
    for b, (ref, j) in enumerate(blocks):
        for c in range(s.chunks):
            rows_ref[b * s.base : (b + 1) * s.base, c * LANES : (c + 1) * LANES] = ref[
                j, c * s.base : (c + 1) * s.base, :
            ]
        tail_ref[b * TAIL : (b + 1) * TAIL, :] = ref[j, s.tail_at : s.block_rows, :]


def sorted_tails(s, tails, blocks, group):
    per = blocks // group
    padded = -(-per // 8) * 8
    used = s.chunks + CLUSTER_DIGITS + RANK_DIGITS
    lines = used * group * padded
    line = iota((lines, blocks * TAIL), 0)
    r = line % padded
    rest = line // padded
    m = rest % group
    field = rest // group
    source = jnp.where(r < per, (r * group + m) * TAIL + field, -1)
    pick = (iota((lines, blocks * TAIL), 1) == source).astype(jnp.float32).astype(jnp.bfloat16)
    picked = dot(pick, tails)
    step = group * padded
    parts = [picked[f * step : (f + 1) * step] for f in range(used)]
    at = s.chunks
    cluster = parts[at] + 256.0 * parts[at + 1]
    at += CLUSTER_DIGITS
    rank = parts[at] + 256.0 * parts[at + 1] + 65536.0 * parts[at + 2]
    return parts[: s.chunks], cluster, rank, padded


def key_lines(s, field, padded, group):
    lane = iota((padded, LANES), 1)
    result = jnp.zeros((padded, LANES), jnp.float32)
    for m in range(group):
        part = jnp.where(lane < s.base, field[m * padded : (m + 1) * padded], 0.0)
        result = result + (pltpu.roll(part, m * s.base, 1) if m else part)
    return result


def load_queries(s, blocks, rows_ref, tail_ref, query_cluster_ref, query_rank_ref):
    n = len(blocks)
    unpack(s, blocks, rows_ref, tail_ref)
    pieces, cluster, rank, _ = sorted_tails(s, tail_ref[: n * TAIL, :], n, 1)
    for field, ref in ((cluster, query_cluster_ref), (rank, query_rank_ref)):
        columns = field.T
        for b in range(n):
            ref[b * s.base : (b + 1) * s.base, :] = jnp.broadcast_to(
                columns[: s.base, b : b + 1], (s.base, LANES)
            )
        if s.extra:
            at = n * s.base
            ref[at : at + n, :] = jnp.broadcast_to(field[:n, s.base : s.base + 1], (n, LANES))
            if s.query_rows > at + n:
                ref[at + n :, :] = jnp.zeros((s.query_rows - at - n, LANES), jnp.float32)
    if s.extra:
        at = n * s.base
        for c, piece in enumerate(pieces):
            spare = s.query_rows - at - piece.shape[0]
            if spare:
                piece = jnp.concatenate([piece, jnp.zeros((spare, LANES), jnp.float32)], axis=0)
            rows_ref[at:, c * LANES : (c + 1) * LANES] = piece.astype(jnp.bfloat16)


def match_keys(s, blocks, keys_ref, tail_ref, queries_ref, query_cluster_ref, query_rank_ref, best):
    n = len(blocks)
    group = s.per_lane_tile
    unpack(s, blocks, keys_ref, tail_ref)
    pieces, cluster, rank, padded = sorted_tails(s, tail_ref[: n * TAIL, :], n, group)
    key_cluster = key_lines(s, cluster, padded, group)
    key_rank = key_lines(s, rank, padded, group)
    queries = queries_ref[...]
    query_cluster = query_cluster_ref[...]
    query_rank = query_rank_ref[...]

    def take(best, scores, line_cluster, line_rank):
        usable = (query_cluster == line_cluster) & (line_rank < query_rank)
        return jnp.maximum(best, jnp.where(usable, scores, -1.0))

    tiles = n // group
    for first in range(0, tiles, 2):
        count = min(2, tiles - first)
        keys = keys_ref[first * LANES : (first + count) * LANES, :]
        scores = dot(queries, keys, ((1,), (1,)))
        for i in range(count):
            t = first + i
            best = take(
                best, scores[:, i * LANES : (i + 1) * LANES], key_cluster[t : t + 1], key_rank[t : t + 1]
            )
    if s.extra:
        count = group * padded
        spare = LANES - count
        for c, piece in enumerate(pieces):
            padded_piece = jnp.concatenate([piece, jnp.zeros((spare, LANES), jnp.float32)], axis=0) if spare else piece
            keys_ref[tiles * LANES :, c * LANES : (c + 1) * LANES] = padded_piece.astype(jnp.bfloat16)
        scores = dot(queries, keys_ref[tiles * LANES :, :], ((1,), (1,)))
        lines = []
        for field in (cluster, rank):
            line = field.T[s.base : s.base + 1, :]
            lines.append(jnp.concatenate([line, jnp.zeros((1, spare), jnp.float32)], axis=1) if spare else line)
        best = take(best, scores, *lines)
    return best


def write_best(s, order, best, out_ref):
    n = s.classes
    column = jnp.max(best, axis=1, keepdims=True)
    eye = iota((s.base, LANES), 0) == iota((s.base, LANES), 1)
    lane = iota((1, LANES), 1)
    me = my_class(s)
    for b, r in enumerate(order):
        line = jnp.sum(jnp.where(eye, column[b * s.base : (b + 1) * s.base], 0.0), axis=0, keepdims=True)
        if s.extra:
            at = n * s.base + b
            line = jnp.where(lane == s.base, column[at : at + 1], line)
        out_ref[pl.ds(me ^ r, 1), :, :] = line[None]


def first_kernel(s, order, query_count, key_count, last, *refs):
    refs = list(refs)
    query_blocks = blocks_of(refs[:query_count])
    key_refs = refs[query_count : query_count + key_count]
    outs = refs[query_count + key_count :]
    queries_ref, query_cluster_ref, query_rank_ref, best_ref, query_tail, keys_ref, key_tail = outs
    load_queries(s, query_blocks, queries_ref, query_tail, query_cluster_ref, query_rank_ref)
    best = jnp.full((s.query_rows, LANES), -1.0, jnp.float32)
    best = match_keys(
        s, query_blocks + blocks_of(key_refs), keys_ref, key_tail, queries_ref, query_cluster_ref, query_rank_ref, best
    )
    if last:
        write_best(s, order, best, best_ref)
    else:
        best_ref[...] = best


def next_kernel(s, order, key_count, last, *refs):
    queries_ref, query_cluster_ref, query_rank_ref, best_ref = refs[:4]
    key_refs = refs[4 : 4 + key_count]
    out_ref, keys_ref, key_tail = refs[4 + key_count :]
    best = match_keys(
        s, blocks_of(key_refs), keys_ref, key_tail, queries_ref, query_cluster_ref, query_rank_ref, best_ref[...]
    )
    if last:
        write_best(s, order, best, out_ref)
    else:
        out_ref[...] = best


def key_scratch(s, blocks):
    rows = blocks * s.base + (LANES if s.extra else 0)
    return [pltpu.VMEM((rows, s.width), jnp.bfloat16), pltpu.VMEM((blocks * TAIL, LANES), jnp.bfloat16)]


def cost(s, blocks):
    keys = blocks * s.base
    return pl.CostEstimate(
        flops=2 * s.query_rows * keys * s.width,
        transcendentals=0,
        bytes_accessed=2 * blocks * s.block_rows * LANES,
    )


def match_first(s, order, queries, keys, last):
    blocks = sum(a.shape[0] for a in queries + keys)
    best_shape = (s.classes, 1, LANES) if last else (s.query_rows, LANES)
    return pl.pallas_call(
        functools.partial(first_kernel, s, order, len(queries), len(keys), last),
        out_shape=[
            jax.ShapeDtypeStruct((s.query_rows, s.width), jnp.bfloat16),
            jax.ShapeDtypeStruct((s.query_rows, LANES), jnp.float32),
            jax.ShapeDtypeStruct((s.query_rows, LANES), jnp.float32),
            jax.ShapeDtypeStruct(best_shape, jnp.float32),
        ],
        scratch_shapes=[pltpu.VMEM((s.classes * TAIL, LANES), jnp.bfloat16)] + key_scratch(s, blocks),
        compiler_params=pltpu.CompilerParams(vmem_limit_bytes=VMEM_LIMIT),
        cost_estimate=cost(s, blocks),
        name="match_first",
    )(*queries, *keys)


def match_next(s, order, state, keys, last):
    blocks = sum(a.shape[0] for a in keys)
    best_shape = (s.classes, 1, LANES) if last else (s.query_rows, LANES)
    best = pl.pallas_call(
        functools.partial(next_kernel, s, order, len(keys), last),
        out_shape=jax.ShapeDtypeStruct(best_shape, jnp.float32),
        scratch_shapes=key_scratch(s, blocks),
        compiler_params=pltpu.CompilerParams(vmem_limit_bytes=VMEM_LIMIT),
        cost_estimate=cost(s, blocks),
        name="match_next",
    )(*state, *keys)
    return [*state[:3], best]


def collect_kernel(s, info_ref, best_ref, out_ref):
    n = s.classes
    best = best_ref[...].reshape(n, LANES)
    parts = []
    for _ in range(3):
        part = best.astype(jnp.bfloat16)
        parts.append(part.astype(jnp.float32))
        best = best - parts[-1]
    target = info_ref[0:1, :]
    within = info_ref[1:2, :]
    pick = (iota((LANES, s.rows), 0) == within).astype(jnp.float32).astype(jnp.bfloat16)
    found = dot(jnp.concatenate(parts, axis=0).astype(jnp.bfloat16), pick)
    found = found[:n] + found[n : 2 * n] + found[2 * n :]
    mine = iota((n, s.rows), 0) == target
    line = jnp.sum(jnp.where(mine, found, 0.0), axis=0, keepdims=True)
    for i in range(s.rows // LANES):
        out_ref[i : i + 1, :] = line[:, i * LANES : (i + 1) * LANES]


def collect(s, info, best):
    out = pl.pallas_call(
        functools.partial(collect_kernel, s),
        out_shape=jax.ShapeDtypeStruct((s.rows // LANES, LANES), jnp.float32),
        name="collect",
    )(info, best)
    return out.reshape(s.rows)


def swap(array, axis, flip):
    size = lax.axis_size(axis)
    return lax.ppermute(array, axis, [(i, i ^ flip) for i in range(size)])


def local(embed, cluster, rank):
    s = Shape(embed.shape[0], embed.shape[1], lax.axis_size("z"), lax.axis_size("x"), lax.axis_size("y"))
    own = [[s.x * k] for k in range(s.z)]
    far = [s.x * k + 1 for k in range(s.z // 2, s.z)]
    near = [s.x * k + 1 for k in range(s.z // 2)]
    info, *arrays = place(s, own + [far, near], embed, cluster, rank)
    owned, (far_rows, near_rows) = arrays[: s.z], arrays[s.z :]
    crossed = jnp.concatenate([swap(near_rows, "x", 1), swap(far_rows, "x", 1)])
    arrived = [
        jnp.concatenate([owned[k], crossed[k : k + 1]]) for k in range(s.z)
    ]
    arrived = [swap(a, "z", k) if k else a for k, a in enumerate(arrived)]
    order = [s.x * k + j for k in range(s.z) for j in range(s.x)]
    if s.y == 2:
        waves = []
        for a in arrived:
            over = swap(a, "y", 1)
            waves.append([swap(a, "core", 1), over, swap(over, "core", 1)])
        state = match_first(s, order, arrived, [], False)
        for i, keys in enumerate(waves):
            if i % 2 == 1:
                state = match_next(s, order, state, waves[i - 1] + keys, i == len(waves) - 1)
    else:
        both = jnp.concatenate(arrived)
        everyone = lax.all_gather(both, ("core", "y"), axis=0)
        state = match_first(s, order, [both], [], False)
        me = lax.axis_index(("core", "y"))
        size = everyone.shape[0]
        for i in range(1, size):
            keys = lax.dynamic_index_in_dim(everyone, (me + i) % size, keepdims=False)
            state = match_next(s, order, state, [keys], i == size - 1)
    returned = lax.all_to_all(state[3], ("z", "x"), split_axis=0, concat_axis=0, tiled=True)
    return collect(s, info, returned)


def solution(mesh):
    store, own = mesh.shape["store"], mesh.shape["own"]
    split = Mesh(mesh.devices.reshape(store // 2, 2, own // 2, 2), ("z", "core", "y", "x"))
    spread = ("z", "core", "y", "x")
    return jax.shard_map(
        local,
        mesh=split,
        in_specs=(P(spread, None), P(spread), P(spread)),
        out_specs=P(spread),
        check_vma=False,
    )
```

```python
import functools
from typing import NamedTuple

import jax
import jax.numpy as jnp
from jax import lax
from jax.experimental import pallas as pl
from jax.experimental.pallas import tpu as pltpu
from jax.sharding import Mesh, PartitionSpec as P

LANES = 128
TAIL = 16
CLUSTER_DIGITS = 2
RANK_DIGITS = 3
VMEM_LIMIT = 48 * 1024 * 1024


class Shape(NamedTuple):
    rows: int
    width: int
    z: int
    x: int
    y: int

    @property
    def classes(self):
        return self.z * self.x

    @property
    def capacity(self):
        return self.rows // self.classes + 1

    @property
    def base(self):
        return max(16, (self.rows // self.classes) // 16 * 16)

    @property
    def extra(self):
        return max(0, self.capacity - self.base)

    @property
    def stride(self):
        return self.base + 8 * self.extra

    @property
    def chunks(self):
        return self.width // LANES

    @property
    def tail_at(self):
        return self.chunks * self.base

    @property
    def block_rows(self):
        return self.tail_at + TAIL

    @property
    def per_lane_tile(self):
        return LANES // self.base

    @property
    def query_rows(self):
        return self.classes * self.base + (-(-self.classes // 16) * 16 if self.extra else 0)


def iota(shape, dim):
    return lax.broadcasted_iota(jnp.int32, shape, dim)


def my_class(s):
    return lax.axis_index("z") * s.x + lax.axis_index("x")


def row_of(ref):
    return jnp.concatenate([ref[i : i + 1, :] for i in range(ref.shape[0])], axis=1)


def dot(left, right, contract=((1,), (0,))):
    return lax.dot_general(left, right, (contract, ((), ())), preferred_element_type=jnp.float32)


def place_kernel(s, layout, embed_hbm, cluster_hbm, rank_hbm, info_ref, *refs):
    out_refs, (embed_ref, cluster_ref, rank_ref, arrival) = refs[: len(layout)], refs[len(layout) :]
    pairs = ((embed_hbm, embed_ref), (cluster_hbm, cluster_ref), (rank_hbm, rank_ref))
    copies = [pltpu.make_async_copy(src, dst, arrival.at[i]) for i, (src, dst) in enumerate(pairs)]
    for copy in copies:
        copy.start()
    for copy in copies:
        copy.wait()
    widened = embed_ref[...].astype(jnp.float32)
    total = jnp.sum(widened * widened, axis=1, keepdims=True)
    unit = (widened * lax.rsqrt(total + 1e-06)).astype(jnp.bfloat16)
    cluster = row_of(cluster_ref)
    rank = row_of(rank_ref)
    n = s.classes
    shift = n.bit_length() - 1
    target = cluster & (n - 1)
    relative = target ^ my_class(s)
    member = (iota((n, s.rows), 0) == relative).astype(jnp.float32)
    earlier = (iota((s.rows, s.rows), 0) < iota((s.rows, s.rows), 1)).astype(jnp.float32)
    before = dot(member.astype(jnp.bfloat16), earlier.astype(jnp.bfloat16))
    within = jnp.sum(before * member, axis=0, keepdims=True).astype(jnp.int32)
    position = relative * s.stride + within
    placed = (iota((n * s.stride, s.rows), 0) == position).astype(jnp.float32).astype(jnp.bfloat16)
    grouped = dot(placed, unit)
    local = (cluster >> shift) + 1
    digits = [(local >> (8 * i)) & 255 for i in range(CLUSTER_DIGITS)]
    digits += [(rank >> (8 * i)) & 255 for i in range(RANK_DIGITS)]
    line = iota((TAIL, s.rows), 0)
    fields = jnp.zeros((TAIL, s.rows), jnp.int32)
    for i, digit in enumerate(digits):
        fields = jnp.where(line == s.chunks + i, digit, fields)
    spread = dot(fields.astype(jnp.float32).astype(jnp.bfloat16), placed, ((1,), (1,)))
    tail_line = iota((TAIL, LANES), 0)
    for ref, members in zip(out_refs, layout):
        for slot, r in enumerate(members):
            at = r * s.stride
            for c in range(s.chunks):
                ref[slot, c * s.base : (c + 1) * s.base, :] = grouped[
                    at : at + s.base, c * LANES : (c + 1) * LANES
                ].astype(jnp.bfloat16)
            tail = jnp.concatenate(
                [spread[:, at : at + s.stride], jnp.zeros((TAIL, LANES - s.stride), jnp.float32)], axis=1
            )
            if s.extra:
                for c in range(s.chunks):
                    piece = grouped[at + s.base : at + s.base + 1, c * LANES : (c + 1) * LANES]
                    tail = jnp.where(tail_line == c, piece, tail)
            ref[slot, s.tail_at : s.block_rows, :] = tail.astype(jnp.bfloat16)
    info_ref[...] = jnp.concatenate([target, within], axis=0)


def place(s, layout, embed, cluster, rank):
    inputs = (embed, cluster.reshape(-1, LANES), rank.reshape(-1, LANES))
    outs = [jax.ShapeDtypeStruct((2, s.rows), jnp.int32)]
    outs += [jax.ShapeDtypeStruct((len(m), s.block_rows, LANES), jnp.bfloat16) for m in layout]
    return pl.pallas_call(
        functools.partial(place_kernel, s, layout),
        out_shape=outs,
        in_specs=[pl.BlockSpec(memory_space=pltpu.HBM)] * 3,
        scratch_shapes=[
            pltpu.VMEM(embed.shape, embed.dtype),
            pltpu.VMEM((s.rows // LANES, LANES), jnp.int32),
            pltpu.VMEM((s.rows // LANES, LANES), jnp.int32),
            pltpu.SemaphoreType.DMA((3,)),
        ],
        compiler_params=pltpu.CompilerParams(vmem_limit_bytes=VMEM_LIMIT),
        name="place",
    )(*(pltpu.with_memory_space_constraint(a, pltpu.HBM) for a in inputs))


def blocks_of(refs):
    return [(ref, j) for ref in refs for j in range(ref.shape[0])]


def unpack(s, blocks, rows_ref, tail_ref):
    for b, (ref, j) in enumerate(blocks):
        for c in range(s.chunks):
            rows_ref[b * s.base : (b + 1) * s.base, c * LANES : (c + 1) * LANES] = ref[
                j, c * s.base : (c + 1) * s.base, :
            ]
        tail_ref[b * TAIL : (b + 1) * TAIL, :] = ref[j, s.tail_at : s.block_rows, :]


def sorted_tails(s, tails, blocks, group):
    per = blocks // group
    padded = -(-per // 8) * 8
    used = s.chunks + CLUSTER_DIGITS + RANK_DIGITS
    lines = used * group * padded
    line = iota((lines, blocks * TAIL), 0)
    r = line % padded
    rest = line // padded
    m = rest % group
    field = rest // group
    source = jnp.where(r < per, (r * group + m) * TAIL + field, -1)
    pick = (iota((lines, blocks * TAIL), 1) == source).astype(jnp.float32).astype(jnp.bfloat16)
    picked = dot(pick, tails)
    step = group * padded
    parts = [picked[f * step : (f + 1) * step] for f in range(used)]
    at = s.chunks
    cluster = parts[at] + 256.0 * parts[at + 1]
    at += CLUSTER_DIGITS
    rank = parts[at] + 256.0 * parts[at + 1] + 65536.0 * parts[at + 2]
    return parts[: s.chunks], cluster, rank, padded


def key_lines(s, field, padded, group):
    lane = iota((padded, LANES), 1)
    result = jnp.zeros((padded, LANES), jnp.float32)
    for m in range(group):
        part = jnp.where(lane < s.base, field[m * padded : (m + 1) * padded], 0.0)
        result = result + (pltpu.roll(part, m * s.base, 1) if m else part)
    return result


def load_queries(s, blocks, rows_ref, tail_ref, query_cluster_ref, query_rank_ref):
    n = len(blocks)
    unpack(s, blocks, rows_ref, tail_ref)
    pieces, cluster, rank, _ = sorted_tails(s, tail_ref[: n * TAIL, :], n, 1)
    for field, ref in ((cluster, query_cluster_ref), (rank, query_rank_ref)):
        columns = field.T
        for b in range(n):
            ref[b * s.base : (b + 1) * s.base, :] = jnp.broadcast_to(
                columns[: s.base, b : b + 1], (s.base, LANES)
            )
        if s.extra:
            at = n * s.base
            ref[at : at + n, :] = jnp.broadcast_to(field[:n, s.base : s.base + 1], (n, LANES))
            if s.query_rows > at + n:
                ref[at + n :, :] = jnp.zeros((s.query_rows - at - n, LANES), jnp.float32)
    if s.extra:
        at = n * s.base
        for c, piece in enumerate(pieces):
            spare = s.query_rows - at - piece.shape[0]
            if spare:
                piece = jnp.concatenate([piece, jnp.zeros((spare, LANES), jnp.float32)], axis=0)
            rows_ref[at:, c * LANES : (c + 1) * LANES] = piece.astype(jnp.bfloat16)


def match_keys(s, blocks, keys_ref, tail_ref, queries_ref, query_cluster_ref, query_rank_ref, best):
    n = len(blocks)
    group = s.per_lane_tile
    unpack(s, blocks, keys_ref, tail_ref)
    pieces, cluster, rank, padded = sorted_tails(s, tail_ref[: n * TAIL, :], n, group)
    key_cluster = key_lines(s, cluster, padded, group)
    key_rank = key_lines(s, rank, padded, group)
    queries = queries_ref[...]
    query_cluster = query_cluster_ref[...]
    query_rank = query_rank_ref[...]

    def take(best, scores, line_cluster, line_rank):
        usable = (query_cluster == line_cluster) & (line_rank < query_rank)
        return jnp.maximum(best, jnp.where(usable, scores, -1.0))

    tiles = n // group
    for first in range(0, tiles, 2):
        count = min(2, tiles - first)
        keys = keys_ref[first * LANES : (first + count) * LANES, :]
        scores = dot(queries, keys, ((1,), (1,)))
        for i in range(count):
            t = first + i
            best = take(
                best, scores[:, i * LANES : (i + 1) * LANES], key_cluster[t : t + 1], key_rank[t : t + 1]
            )
    if s.extra:
        count = group * padded
        spare = LANES - count
        for c, piece in enumerate(pieces):
            padded_piece = jnp.concatenate([piece, jnp.zeros((spare, LANES), jnp.float32)], axis=0) if spare else piece
            keys_ref[tiles * LANES :, c * LANES : (c + 1) * LANES] = padded_piece.astype(jnp.bfloat16)
        scores = dot(queries, keys_ref[tiles * LANES :, :], ((1,), (1,)))
        lines = []
        for field in (cluster, rank):
            line = field.T[s.base : s.base + 1, :]
            lines.append(jnp.concatenate([line, jnp.zeros((1, spare), jnp.float32)], axis=1) if spare else line)
        best = take(best, scores, *lines)
    return best


def write_best(s, order, best, out_ref):
    n = s.classes
    column = jnp.max(best, axis=1, keepdims=True)
    eye = iota((s.base, LANES), 0) == iota((s.base, LANES), 1)
    lane = iota((1, LANES), 1)
    me = my_class(s)
    for b, r in enumerate(order):
        line = jnp.sum(jnp.where(eye, column[b * s.base : (b + 1) * s.base], 0.0), axis=0, keepdims=True)
        if s.extra:
            at = n * s.base + b
            line = jnp.where(lane == s.base, column[at : at + 1], line)
        out_ref[pl.ds(me ^ r, 1), :, :] = line[None]


def first_kernel(s, order, query_count, key_count, last, *refs):
    refs = list(refs)
    query_blocks = blocks_of(refs[:query_count])
    key_refs = refs[query_count : query_count + key_count]
    outs = refs[query_count + key_count :]
    queries_ref, query_cluster_ref, query_rank_ref, best_ref, query_tail, keys_ref, key_tail = outs
    load_queries(s, query_blocks, queries_ref, query_tail, query_cluster_ref, query_rank_ref)
    best = jnp.full((s.query_rows, LANES), -1.0, jnp.float32)
    best = match_keys(
        s, query_blocks + blocks_of(key_refs), keys_ref, key_tail, queries_ref, query_cluster_ref, query_rank_ref, best
    )
    if last:
        write_best(s, order, best, best_ref)
    else:
        best_ref[...] = best


def next_kernel(s, order, key_count, last, *refs):
    queries_ref, query_cluster_ref, query_rank_ref, best_ref = refs[:4]
    key_refs = refs[4 : 4 + key_count]
    out_ref, keys_ref, key_tail = refs[4 + key_count :]
    best = match_keys(
        s, blocks_of(key_refs), keys_ref, key_tail, queries_ref, query_cluster_ref, query_rank_ref, best_ref[...]
    )
    if last:
        write_best(s, order, best, out_ref)
    else:
        out_ref[...] = best


def key_scratch(s, blocks):
    rows = blocks * s.base + (LANES if s.extra else 0)
    return [pltpu.VMEM((rows, s.width), jnp.bfloat16), pltpu.VMEM((blocks * TAIL, LANES), jnp.bfloat16)]


def cost(s, blocks):
    keys = blocks * s.base
    return pl.CostEstimate(
        flops=2 * s.query_rows * keys * s.width,
        transcendentals=0,
        bytes_accessed=2 * blocks * s.block_rows * LANES,
    )


def match_first(s, order, queries, keys, last):
    blocks = sum(a.shape[0] for a in queries + keys)
    best_shape = (s.classes, 1, LANES) if last else (s.query_rows, LANES)
    return pl.pallas_call(
        functools.partial(first_kernel, s, order, len(queries), len(keys), last),
        out_shape=[
            jax.ShapeDtypeStruct((s.query_rows, s.width), jnp.bfloat16),
            jax.ShapeDtypeStruct((s.query_rows, LANES), jnp.float32),
            jax.ShapeDtypeStruct((s.query_rows, LANES), jnp.float32),
            jax.ShapeDtypeStruct(best_shape, jnp.float32),
        ],
        scratch_shapes=[pltpu.VMEM((s.classes * TAIL, LANES), jnp.bfloat16)] + key_scratch(s, blocks),
        compiler_params=pltpu.CompilerParams(vmem_limit_bytes=VMEM_LIMIT),
        cost_estimate=cost(s, blocks),
        name="match_first",
    )(*queries, *keys)


def match_next(s, order, state, keys, last):
    blocks = sum(a.shape[0] for a in keys)
    best_shape = (s.classes, 1, LANES) if last else (s.query_rows, LANES)
    best = pl.pallas_call(
        functools.partial(next_kernel, s, order, len(keys), last),
        out_shape=jax.ShapeDtypeStruct(best_shape, jnp.float32),
        scratch_shapes=key_scratch(s, blocks),
        compiler_params=pltpu.CompilerParams(vmem_limit_bytes=VMEM_LIMIT),
        cost_estimate=cost(s, blocks),
        name="match_next",
    )(*state, *keys)
    return [*state[:3], best]


def collect_kernel(s, info_ref, best_ref, out_ref):
    n = s.classes
    best = best_ref[...].reshape(n, LANES)
    parts = []
    for _ in range(3):
        part = best.astype(jnp.bfloat16)
        parts.append(part.astype(jnp.float32))
        best = best - parts[-1]
    target = info_ref[0:1, :]
    within = info_ref[1:2, :]
    pick = (iota((LANES, s.rows), 0) == within).astype(jnp.float32).astype(jnp.bfloat16)
    found = dot(jnp.concatenate(parts, axis=0).astype(jnp.bfloat16), pick)
    found = found[:n] + found[n : 2 * n] + found[2 * n :]
    mine = iota((n, s.rows), 0) == target
    line = jnp.sum(jnp.where(mine, found, 0.0), axis=0, keepdims=True)
    for i in range(s.rows // LANES):
        out_ref[i : i + 1, :] = line[:, i * LANES : (i + 1) * LANES]


def collect(s, info, best):
    out = pl.pallas_call(
        functools.partial(collect_kernel, s),
        out_shape=jax.ShapeDtypeStruct((s.rows // LANES, LANES), jnp.float32),
        compiler_params=pltpu.CompilerParams(vmem_limit_bytes=8 * 1024 * 1024),
        name="collect",
    )(info, best)
    return out.reshape(s.rows)


def swap(array, axis, flip):
    size = lax.axis_size(axis)
    return lax.ppermute(array, axis, [(i, i ^ flip) for i in range(size)])


def local(embed, cluster, rank):
    s = Shape(embed.shape[0], embed.shape[1], lax.axis_size("z"), lax.axis_size("x"), lax.axis_size("y"))
    order = [s.x * k + j for k in range(s.z) for j in range(s.x)]
    info, *blocks = place(s, [[s.x * k + j for j in range(s.x)] for k in range(s.z)], embed, cluster, rank)
    arrived = {k: swap(blocks[k], "z", k) if k else blocks[k] for k in reversed(range(s.z))}
    near = swap(jnp.concatenate([arrived[0][1:], arrived[1][1:]]), "x", 1)
    queries = [jnp.concatenate([arrived[0][:1], near[:1], arrived[1][:1], near[1:]])]
    queries += [jnp.concatenate([arrived[k][:1], swap(arrived[k][1:], "x", 1)]) for k in range(2, s.z)]
    state = match_first(s, order, queries, [], False)
    if s.y == 2:
        waves = []
        for a in queries:
            over = swap(a, "y", 1)
            waves.append([over, swap(jnp.concatenate([a, over]), "core", 1)])
        state = match_next(s, order, state, waves[0], False)
        state = match_next(s, order, state, [a for wave in waves[1:] for a in wave], True)
    else:
        everyone = lax.all_gather(jnp.concatenate(queries), ("core", "y"), axis=0)
        me = lax.axis_index(("core", "y"))
        size = everyone.shape[0]
        for i in range(1, size):
            keys = lax.dynamic_index_in_dim(everyone, (me + i) % size, keepdims=False)
            state = match_next(s, order, state, [keys], i == size - 1)
    returned = lax.all_to_all(state[3], ("z", "x"), split_axis=0, concat_axis=0, tiled=True)
    return collect(s, info, returned)


def solution(mesh):
    store, own = mesh.shape["store"], mesh.shape["own"]
    split = Mesh(mesh.devices.reshape(store // 2, 2, own // 2, 2), ("z", "core", "y", "x"))
    spread = ("z", "core", "y", "x")
    return jax.shard_map(
        local,
        mesh=split,
        in_specs=(P(spread, None), P(spread), P(spread)),
        out_specs=P(spread),
        check_vma=False,
    )
```

```python
import functools
from typing import NamedTuple

import jax
import jax.numpy as jnp
from jax import lax
from jax.experimental import pallas as pl
from jax.experimental.pallas import tpu as pltpu
from jax.sharding import Mesh, PartitionSpec as P

LANES = 128
TAIL = 16
CLUSTER_DIGITS = 2
RANK_DIGITS = 3
FETCHES = 1
VMEM_LIMIT = 48 * 1024 * 1024


class Shape(NamedTuple):
    rows: int
    width: int
    z: int
    x: int
    y: int

    @property
    def classes(self):
        return self.z * self.x

    @property
    def capacity(self):
        return self.rows // self.classes + 1

    @property
    def base(self):
        return max(16, (self.rows // self.classes) // 16 * 16)

    @property
    def extra(self):
        return max(0, self.capacity - self.base)

    @property
    def stride(self):
        return self.base + 8 * self.extra

    @property
    def chunks(self):
        return self.width // LANES

    @property
    def tail_at(self):
        return self.chunks * self.base

    @property
    def block_rows(self):
        return self.tail_at + TAIL

    @property
    def per_lane_tile(self):
        return LANES // self.base

    @property
    def query_rows(self):
        return self.classes * self.base + (-(-self.classes // 16) * 16 if self.extra else 0)


def iota(shape, dim):
    return lax.broadcasted_iota(jnp.int32, shape, dim)


def my_class(s):
    return lax.axis_index("z") * s.x + lax.axis_index("x")


def row_of(ref):
    return jnp.concatenate([ref[i : i + 1, :] for i in range(ref.shape[0])], axis=1)


def dot(left, right, contract=((1,), (0,))):
    return lax.dot_general(left, right, (contract, ((), ())), preferred_element_type=jnp.float32)


def place_kernel(s, layout, embed_hbm, cluster_hbm, rank_hbm, info_ref, *refs):
    out_refs, (embed_ref, cluster_ref, rank_ref, arrival) = refs[: len(layout)], refs[len(layout) :]
    part = s.rows // FETCHES
    pairs = [(cluster_hbm, cluster_ref), (rank_hbm, rank_ref)]
    pairs += [(embed_hbm.at[pl.ds(i * part, part)], embed_ref.at[pl.ds(i * part, part)]) for i in range(FETCHES)]
    copies = [pltpu.make_async_copy(src, dst, arrival.at[i]) for i, (src, dst) in enumerate(pairs)]
    for copy in copies:
        copy.start()
    for copy in copies[:2]:
        copy.wait()
    cluster = row_of(cluster_ref)
    rank = row_of(rank_ref)
    n = s.classes
    shift = n.bit_length() - 1
    target = cluster & (n - 1)
    relative = target ^ my_class(s)
    member = (iota((n, s.rows), 0) == relative).astype(jnp.float32)
    earlier = (iota((s.rows, s.rows), 0) < iota((s.rows, s.rows), 1)).astype(jnp.float32)
    before = dot(member.astype(jnp.bfloat16), earlier.astype(jnp.bfloat16))
    within = jnp.sum(before * member, axis=0, keepdims=True).astype(jnp.int32)
    position = relative * s.stride + within
    placed = (iota((n * s.stride, s.rows), 0) == position).astype(jnp.float32).astype(jnp.bfloat16)
    local = (cluster >> shift) + 1
    digits = [(local >> (8 * i)) & 255 for i in range(CLUSTER_DIGITS)]
    digits += [(rank >> (8 * i)) & 255 for i in range(RANK_DIGITS)]
    line = iota((TAIL, s.rows), 0)
    fields = jnp.zeros((TAIL, s.rows), jnp.int32)
    for i, digit in enumerate(digits):
        fields = jnp.where(line == s.chunks + i, digit, fields)
    spread = dot(fields.astype(jnp.float32).astype(jnp.bfloat16), placed, ((1,), (1,)))
    for copy in copies[2:]:
        copy.wait()
    widened = embed_ref[...].astype(jnp.float32)
    total = jnp.sum(widened * widened, axis=1, keepdims=True)
    unit = (widened * lax.rsqrt(total + 1e-06)).astype(jnp.bfloat16)
    grouped = dot(placed, unit)
    tail_line = iota((TAIL, LANES), 0)
    for ref, members in zip(out_refs, layout):
        for slot, r in enumerate(members):
            at = r * s.stride
            for c in range(s.chunks):
                ref[slot, c * s.base : (c + 1) * s.base, :] = grouped[
                    at : at + s.base, c * LANES : (c + 1) * LANES
                ].astype(jnp.bfloat16)
            tail = jnp.concatenate(
                [spread[:, at : at + s.stride], jnp.zeros((TAIL, LANES - s.stride), jnp.float32)], axis=1
            )
            if s.extra:
                for c in range(s.chunks):
                    piece = grouped[at + s.base : at + s.base + 1, c * LANES : (c + 1) * LANES]
                    tail = jnp.where(tail_line == c, piece, tail)
            ref[slot, s.tail_at : s.block_rows, :] = tail.astype(jnp.bfloat16)
    info_ref[...] = jnp.concatenate([target, within], axis=0)


def place(s, layout, embed, cluster, rank):
    inputs = (embed, cluster.reshape(-1, LANES), rank.reshape(-1, LANES))
    outs = [jax.ShapeDtypeStruct((2, s.rows), jnp.int32)]
    outs += [jax.ShapeDtypeStruct((len(m), s.block_rows, LANES), jnp.bfloat16) for m in layout]
    return pl.pallas_call(
        functools.partial(place_kernel, s, layout),
        out_shape=outs,
        in_specs=[pl.BlockSpec(memory_space=pltpu.HBM)] * 3,
        scratch_shapes=[
            pltpu.VMEM(embed.shape, embed.dtype),
            pltpu.VMEM((s.rows // LANES, LANES), jnp.int32),
            pltpu.VMEM((s.rows // LANES, LANES), jnp.int32),
            pltpu.SemaphoreType.DMA((2 + FETCHES,)),
        ],
        compiler_params=pltpu.CompilerParams(vmem_limit_bytes=VMEM_LIMIT),
        name="place",
    )(*(pltpu.with_memory_space_constraint(a, pltpu.HBM) for a in inputs))


def blocks_of(refs):
    return [(ref, j) for ref in refs for j in range(ref.shape[0])]


def unpack(s, blocks, rows_ref, tail_ref):
    for b, (ref, j) in enumerate(blocks):
        for c in range(s.chunks):
            rows_ref[b * s.base : (b + 1) * s.base, c * LANES : (c + 1) * LANES] = ref[
                j, c * s.base : (c + 1) * s.base, :
            ]
        tail_ref[b * TAIL : (b + 1) * TAIL, :] = ref[j, s.tail_at : s.block_rows, :]


def split(value, by):
    if by & (by - 1):
        return value // by, value % by
    return value >> (by.bit_length() - 1), value & (by - 1)


def sorted_tails(s, tails, blocks, group):
    per = blocks // group
    padded = -(-per // 8) * 8
    used = s.chunks + CLUSTER_DIGITS + RANK_DIGITS
    lines = used * group * padded
    line = iota((lines, blocks * TAIL), 0)
    rest, r = split(line, padded)
    field, m = split(rest, group)
    source = jnp.where(r < per, (r * group + m) * TAIL + field, -1)
    pick = (iota((lines, blocks * TAIL), 1) == source).astype(jnp.float32).astype(jnp.bfloat16)
    picked = dot(pick, tails)
    step = group * padded
    parts = [picked[f * step : (f + 1) * step] for f in range(used)]
    at = s.chunks
    cluster = parts[at] + 256.0 * parts[at + 1]
    at += CLUSTER_DIGITS
    rank = parts[at] + 256.0 * parts[at + 1] + 65536.0 * parts[at + 2]
    return parts[: s.chunks], cluster, rank, padded


def key_lines(s, field, padded, group):
    lane = iota((padded, LANES), 1)
    result = jnp.zeros((padded, LANES), jnp.float32)
    for m in range(group):
        part = jnp.where(lane < s.base, field[m * padded : (m + 1) * padded], 0.0)
        result = result + (pltpu.roll(part, m * s.base, 1) if m else part)
    return result


def load_queries(s, blocks, rows_ref, tail_ref, query_cluster_ref, query_rank_ref):
    n = len(blocks)
    unpack(s, blocks, rows_ref, tail_ref)
    pieces, cluster, rank, _ = sorted_tails(s, tail_ref[: n * TAIL, :], n, 1)
    for field, ref in ((cluster, query_cluster_ref), (rank, query_rank_ref)):
        columns = field.T
        for b in range(n):
            ref[b * s.base : (b + 1) * s.base, :] = jnp.broadcast_to(
                columns[: s.base, b : b + 1], (s.base, LANES)
            )
        if s.extra:
            at = n * s.base
            ref[at : at + n, :] = jnp.broadcast_to(field[:n, s.base : s.base + 1], (n, LANES))
            if s.query_rows > at + n:
                ref[at + n :, :] = jnp.zeros((s.query_rows - at - n, LANES), jnp.float32)
    if s.extra:
        at = n * s.base
        for c, piece in enumerate(pieces):
            spare = s.query_rows - at - piece.shape[0]
            if spare:
                piece = jnp.concatenate([piece, jnp.zeros((spare, LANES), jnp.float32)], axis=0)
            rows_ref[at:, c * LANES : (c + 1) * LANES] = piece.astype(jnp.bfloat16)


def match_keys(s, blocks, keys_ref, tail_ref, queries_ref, query_cluster_ref, query_rank_ref, best):
    n = len(blocks)
    group = s.per_lane_tile
    unpack(s, blocks, keys_ref, tail_ref)
    pieces, cluster, rank, padded = sorted_tails(s, tail_ref[: n * TAIL, :], n, group)
    key_cluster = key_lines(s, cluster, padded, group)
    key_rank = key_lines(s, rank, padded, group)
    queries = queries_ref[...]
    query_cluster = query_cluster_ref[...]
    query_rank = query_rank_ref[...]

    def take(best, scores, line_cluster, line_rank):
        usable = (query_cluster == line_cluster) & (line_rank < query_rank)
        return jnp.maximum(best, jnp.where(usable, scores, -1.0))

    tiles = n // group
    for first in range(0, tiles, 2):
        count = min(2, tiles - first)
        keys = keys_ref[first * LANES : (first + count) * LANES, :]
        scores = dot(queries, keys, ((1,), (1,)))
        for i in range(count):
            t = first + i
            best = take(
                best, scores[:, i * LANES : (i + 1) * LANES], key_cluster[t : t + 1], key_rank[t : t + 1]
            )
    if s.extra:
        count = group * padded
        spare = LANES - count
        for c, piece in enumerate(pieces):
            padded_piece = jnp.concatenate([piece, jnp.zeros((spare, LANES), jnp.float32)], axis=0) if spare else piece
            keys_ref[tiles * LANES :, c * LANES : (c + 1) * LANES] = padded_piece.astype(jnp.bfloat16)
        scores = dot(queries, keys_ref[tiles * LANES :, :], ((1,), (1,)))
        lines = []
        for field in (cluster, rank):
            line = field.T[s.base : s.base + 1, :]
            lines.append(jnp.concatenate([line, jnp.zeros((1, spare), jnp.float32)], axis=1) if spare else line)
        best = take(best, scores, *lines)
    return best


def write_best(s, order, best, out_ref):
    n = s.classes
    column = jnp.max(best, axis=1, keepdims=True)
    eye = iota((s.base, LANES), 0) == iota((s.base, LANES), 1)
    lane = iota((1, LANES), 1)
    me = my_class(s)
    for b, r in enumerate(order):
        line = jnp.sum(jnp.where(eye, column[b * s.base : (b + 1) * s.base], 0.0), axis=0, keepdims=True)
        if s.extra:
            at = n * s.base + b
            line = jnp.where(lane == s.base, column[at : at + 1], line)
        out_ref[pl.ds(me ^ r, 1), :, :] = line[None]


def first_kernel(s, order, query_count, key_count, last, *refs):
    refs = list(refs)
    query_blocks = blocks_of(refs[:query_count])
    key_refs = refs[query_count : query_count + key_count]
    outs = refs[query_count + key_count :]
    queries_ref, query_cluster_ref, query_rank_ref, best_ref, query_tail, keys_ref, key_tail = outs
    load_queries(s, query_blocks, queries_ref, query_tail, query_cluster_ref, query_rank_ref)
    best = jnp.full((s.query_rows, LANES), -1.0, jnp.float32)
    best = match_keys(
        s, query_blocks + blocks_of(key_refs), keys_ref, key_tail, queries_ref, query_cluster_ref, query_rank_ref, best
    )
    if last:
        write_best(s, order, best, best_ref)
    else:
        best_ref[...] = best


def next_kernel(s, order, key_count, last, *refs):
    queries_ref, query_cluster_ref, query_rank_ref, best_ref = refs[:4]
    key_refs = refs[4 : 4 + key_count]
    out_ref, keys_ref, key_tail = refs[4 + key_count :]
    best = match_keys(
        s, blocks_of(key_refs), keys_ref, key_tail, queries_ref, query_cluster_ref, query_rank_ref, best_ref[...]
    )
    if last:
        write_best(s, order, best, out_ref)
    else:
        out_ref[...] = best


def key_scratch(s, blocks):
    rows = blocks * s.base + (LANES if s.extra else 0)
    return [pltpu.VMEM((rows, s.width), jnp.bfloat16), pltpu.VMEM((blocks * TAIL, LANES), jnp.bfloat16)]


def cost(s, blocks):
    keys = blocks * s.base
    return pl.CostEstimate(
        flops=2 * s.query_rows * keys * s.width,
        transcendentals=0,
        bytes_accessed=2 * blocks * s.block_rows * LANES,
    )


def match_first(s, order, queries, keys, last):
    blocks = sum(a.shape[0] for a in queries + keys)
    best_shape = (s.classes, 1, LANES) if last else (s.query_rows, LANES)
    return pl.pallas_call(
        functools.partial(first_kernel, s, order, len(queries), len(keys), last),
        out_shape=[
            jax.ShapeDtypeStruct((s.query_rows, s.width), jnp.bfloat16),
            jax.ShapeDtypeStruct((s.query_rows, LANES), jnp.float32),
            jax.ShapeDtypeStruct((s.query_rows, LANES), jnp.float32),
            jax.ShapeDtypeStruct(best_shape, jnp.float32),
        ],
        scratch_shapes=[pltpu.VMEM((s.classes * TAIL, LANES), jnp.bfloat16)] + key_scratch(s, blocks),
        compiler_params=pltpu.CompilerParams(vmem_limit_bytes=VMEM_LIMIT),
        cost_estimate=cost(s, blocks),
        name="match_first",
    )(*queries, *keys)


def match_next(s, order, state, keys, last):
    blocks = sum(a.shape[0] for a in keys)
    best_shape = (s.classes, 1, LANES) if last else (s.query_rows, LANES)
    best = pl.pallas_call(
        functools.partial(next_kernel, s, order, len(keys), last),
        out_shape=jax.ShapeDtypeStruct(best_shape, jnp.float32),
        scratch_shapes=key_scratch(s, blocks),
        compiler_params=pltpu.CompilerParams(vmem_limit_bytes=VMEM_LIMIT),
        cost_estimate=cost(s, blocks),
        name="match_next",
    )(*state, *keys)
    return [*state[:3], best]


def collect_kernel(s, info_ref, best_ref, out_ref):
    n = s.classes
    best = best_ref[...].reshape(n, LANES)
    parts = []
    for _ in range(3):
        part = best.astype(jnp.bfloat16)
        parts.append(part.astype(jnp.float32))
        best = best - parts[-1]
    target = info_ref[0:1, :]
    within = info_ref[1:2, :]
    pick = (iota((LANES, s.rows), 0) == within).astype(jnp.float32).astype(jnp.bfloat16)
    found = dot(jnp.concatenate(parts, axis=0).astype(jnp.bfloat16), pick)
    found = found[:n] + found[n : 2 * n] + found[2 * n :]
    mine = iota((n, s.rows), 0) == target
    line = jnp.sum(jnp.where(mine, found, 0.0), axis=0, keepdims=True)
    for i in range(s.rows // LANES):
        out_ref[i : i + 1, :] = line[:, i * LANES : (i + 1) * LANES]


def collect(s, info, best):
    out = pl.pallas_call(
        functools.partial(collect_kernel, s),
        out_shape=jax.ShapeDtypeStruct((s.rows // LANES, LANES), jnp.float32),
        compiler_params=pltpu.CompilerParams(vmem_limit_bytes=8 * 1024 * 1024),
        name="collect",
    )(info, best)
    return out.reshape(s.rows)


def swap(array, axis, flip):
    size = lax.axis_size(axis)
    return lax.ppermute(array, axis, [(i, i ^ flip) for i in range(size)])


def local(embed, cluster, rank):
    s = Shape(embed.shape[0], embed.shape[1], lax.axis_size("z"), lax.axis_size("x"), lax.axis_size("y"))
    order = [s.x * k + j for k in range(s.z) for j in range(s.x)]
    info, *blocks = place(s, [[s.x * k + j for j in range(s.x)] for k in range(s.z)], embed, cluster, rank)
    arrived = {k: swap(blocks[k], "z", k) if k else blocks[k] for k in reversed(range(s.z))}
    near = swap(jnp.concatenate([arrived[0][1:], arrived[1][1:]]), "x", 1)
    queries = [jnp.concatenate([arrived[0][:1], near[:1], arrived[1][:1], near[1:]])]
    queries += [jnp.concatenate([arrived[k][:1], swap(arrived[k][1:], "x", 1)]) for k in range(2, s.z)]
    state = match_first(s, order, queries, [], False)
    if s.y == 2:
        waves = []
        for a in queries:
            over = swap(a, "y", 1)
            waves.append([over, swap(jnp.concatenate([a, over]), "core", 1)])
        state = match_next(s, order, state, [wave[0] for wave in waves] + [waves[0][1]], False)
        state = match_next(s, order, state, [wave[1] for wave in waves[1:]], True)
    else:
        everyone = lax.all_gather(jnp.concatenate(queries), ("core", "y"), axis=0)
        me = lax.axis_index(("core", "y"))
        size = everyone.shape[0]
        for i in range(1, size):
            keys = lax.dynamic_index_in_dim(everyone, (me + i) % size, keepdims=False)
            state = match_next(s, order, state, [keys], i == size - 1)
    returned = lax.all_to_all(state[3], ("z", "x"), split_axis=0, concat_axis=0, tiled=True)
    return collect(s, info, returned)


def solution(mesh):
    store, own = mesh.shape["store"], mesh.shape["own"]
    split = Mesh(mesh.devices.reshape(store // 2, 2, own // 2, 2), ("z", "core", "y", "x"))
    spread = ("z", "core", "y", "x")
    return jax.shard_map(
        local,
        mesh=split,
        in_specs=(P(spread, None), P(spread), P(spread)),
        out_specs=P(spread),
        check_vma=False,
    )
```

```python
import functools
from typing import NamedTuple

import jax
import jax.numpy as jnp
from jax import lax
from jax.experimental import pallas as pl
from jax.experimental.pallas import tpu as pltpu
from jax.sharding import Mesh, PartitionSpec as P

LANES = 128
TAIL = 8
FIELD_LINES = 16
PER_LINE = 3
CLUSTER_DIGITS = 2
RANK_DIGITS = 3
FETCHES = 1
VMEM_LIMIT = 48 * 1024 * 1024


class Shape(NamedTuple):
    rows: int
    width: int
    z: int
    x: int
    y: int

    @property
    def classes(self):
        return self.z * self.x

    @property
    def capacity(self):
        return self.rows // self.classes + 1

    @property
    def base(self):
        return max(16, (self.rows // self.classes) // 16 * 16)

    @property
    def extra(self):
        return max(0, self.capacity - self.base)

    @property
    def stride(self):
        return self.base + 8 * self.extra

    @property
    def chunks(self):
        return self.width // LANES

    @property
    def tail_at(self):
        return self.chunks * self.base

    @property
    def block_rows(self):
        return self.tail_at + TAIL

    @property
    def per_lane_tile(self):
        return LANES // self.base

    @property
    def query_rows(self):
        return self.classes * self.base + (-(-self.classes // 16) * 16 if self.extra else 0)


def iota(shape, dim):
    return lax.broadcasted_iota(jnp.int32, shape, dim)


def my_class(s):
    return lax.axis_index("z") * s.x + lax.axis_index("x")


def row_of(ref):
    return jnp.concatenate([ref[i : i + 1, :] for i in range(ref.shape[0])], axis=1)


def dot(left, right, contract=((1,), (0,))):
    return lax.dot_general(left, right, (contract, ((), ())), preferred_element_type=jnp.float32)


def place_kernel(s, layout, embed_hbm, cluster_hbm, rank_hbm, info_ref, *refs):
    out_refs, (embed_ref, cluster_ref, rank_ref, arrival) = refs[: len(layout)], refs[len(layout) :]
    part = s.rows // FETCHES
    pairs = [(cluster_hbm, cluster_ref), (rank_hbm, rank_ref)]
    pairs += [(embed_hbm.at[pl.ds(i * part, part)], embed_ref.at[pl.ds(i * part, part)]) for i in range(FETCHES)]
    copies = [pltpu.make_async_copy(src, dst, arrival.at[i]) for i, (src, dst) in enumerate(pairs)]
    for copy in copies:
        copy.start()
    for copy in copies[:2]:
        copy.wait()
    cluster = row_of(cluster_ref)
    rank = row_of(rank_ref)
    n = s.classes
    shift = n.bit_length() - 1
    target = cluster & (n - 1)
    relative = target ^ my_class(s)
    member = (iota((n, s.rows), 0) == relative).astype(jnp.float32)
    earlier = (iota((s.rows, s.rows), 0) < iota((s.rows, s.rows), 1)).astype(jnp.float32)
    before = dot(member.astype(jnp.bfloat16), earlier.astype(jnp.bfloat16))
    within = jnp.sum(before * member, axis=0, keepdims=True).astype(jnp.int32)
    position = relative * s.stride + within
    placed = (iota((n * s.stride, s.rows), 0) == position).astype(jnp.float32).astype(jnp.bfloat16)
    local = (cluster >> shift) + 1
    digits = [(local >> (8 * i)) & 255 for i in range(CLUSTER_DIGITS)]
    digits += [(rank >> (8 * i)) & 255 for i in range(RANK_DIGITS)]
    line = iota((FIELD_LINES, s.rows), 0)
    fields = jnp.zeros((FIELD_LINES, s.rows), jnp.int32)
    for i, digit in enumerate(digits):
        fields = jnp.where(line == i, digit, fields)
    spread = dot(fields.astype(jnp.float32).astype(jnp.bfloat16), placed, ((1,), (1,)))
    for copy in copies[2:]:
        copy.wait()
    widened = embed_ref[...].astype(jnp.float32)
    total = jnp.sum(widened * widened, axis=1, keepdims=True)
    unit = (widened * lax.rsqrt(total + 1e-06)).astype(jnp.bfloat16)
    grouped = dot(placed, unit)
    tail_line = iota((TAIL, LANES), 0)
    for ref, members in zip(out_refs, layout):
        for slot, r in enumerate(members):
            at = r * s.stride
            for c in range(s.chunks):
                ref[slot, c * s.base : (c + 1) * s.base, :] = grouped[
                    at : at + s.base, c * LANES : (c + 1) * LANES
                ].astype(jnp.bfloat16)
            tail = jnp.zeros((TAIL, LANES), jnp.float32)
            for i in range(0, len(digits), PER_LINE):
                parts = [spread[f : f + 1, at : at + s.stride] for f in range(i, i + PER_LINE)]
                parts.append(jnp.zeros((1, LANES - PER_LINE * s.stride), jnp.float32))
                tail = jnp.where(
                    tail_line == s.chunks + i // PER_LINE, jnp.concatenate(parts, axis=1), tail
                )
            if s.extra:
                for c in range(s.chunks):
                    piece = grouped[at + s.base : at + s.base + 1, c * LANES : (c + 1) * LANES]
                    tail = jnp.where(tail_line == c, piece, tail)
            ref[slot, s.tail_at : s.block_rows, :] = tail.astype(jnp.bfloat16)
    info_ref[...] = jnp.concatenate([target, within], axis=0)


def place(s, layout, embed, cluster, rank):
    inputs = (embed, cluster.reshape(-1, LANES), rank.reshape(-1, LANES))
    outs = [jax.ShapeDtypeStruct((2, s.rows), jnp.int32)]
    outs += [jax.ShapeDtypeStruct((len(m), s.block_rows, LANES), jnp.bfloat16) for m in layout]
    return pl.pallas_call(
        functools.partial(place_kernel, s, layout),
        out_shape=outs,
        in_specs=[pl.BlockSpec(memory_space=pltpu.HBM)] * 3,
        scratch_shapes=[
            pltpu.VMEM(embed.shape, embed.dtype),
            pltpu.VMEM((s.rows // LANES, LANES), jnp.int32),
            pltpu.VMEM((s.rows // LANES, LANES), jnp.int32),
            pltpu.SemaphoreType.DMA((2 + FETCHES,)),
        ],
        compiler_params=pltpu.CompilerParams(vmem_limit_bytes=VMEM_LIMIT),
        name="place",
    )(*(pltpu.with_memory_space_constraint(a, pltpu.HBM) for a in inputs))


def blocks_of(refs):
    return [(ref, j) for ref in refs for j in range(ref.shape[0])]


def unpack(s, blocks, rows_ref, tail_ref):
    for b, (ref, j) in enumerate(blocks):
        for c in range(s.chunks):
            rows_ref[b * s.base : (b + 1) * s.base, c * LANES : (c + 1) * LANES] = ref[
                j, c * s.base : (c + 1) * s.base, :
            ]
        tail_ref[b * TAIL : (b + 1) * TAIL, :] = ref[j, s.tail_at : s.block_rows, :]


def split(value, by):
    if by & (by - 1):
        return value // by, value % by
    return value >> (by.bit_length() - 1), value & (by - 1)


def sorted_tails(s, tails, blocks, group):
    per = blocks // group
    padded = -(-per // 8) * 8
    used = s.chunks - (-(CLUSTER_DIGITS + RANK_DIGITS) // PER_LINE)
    lines = used * group * padded
    line = iota((lines, blocks * TAIL), 0)
    rest, r = split(line, padded)
    field, m = split(rest, group)
    source = jnp.where(r < per, (r * group + m) * TAIL + field, -1)
    pick = (iota((lines, blocks * TAIL), 1) == source).astype(jnp.float32).astype(jnp.bfloat16)
    picked = dot(pick, tails)
    step = group * padded
    parts = [picked[f * step : (f + 1) * step] for f in range(used)]
    digits = []
    for i in range(CLUSTER_DIGITS + RANK_DIGITS):
        digit = parts[s.chunks + i // PER_LINE]
        lane = i % PER_LINE * s.stride
        digits.append(pltpu.roll(digit, LANES - lane, 1) if lane else digit)
    cluster = digits[0] + 256.0 * digits[1]
    rank = digits[2] + 256.0 * digits[3] + 65536.0 * digits[4]
    return parts[: s.chunks], cluster, rank, padded


def key_lines(s, field, padded, group):
    lane = iota((padded, LANES), 1)
    result = jnp.zeros((padded, LANES), jnp.float32)
    for m in range(group):
        part = jnp.where(lane < s.base, field[m * padded : (m + 1) * padded], 0.0)
        result = result + (pltpu.roll(part, m * s.base, 1) if m else part)
    return result


def load_queries(s, blocks, rows_ref, tail_ref, query_cluster_ref, query_rank_ref):
    n = len(blocks)
    unpack(s, blocks, rows_ref, tail_ref)
    pieces, cluster, rank, _ = sorted_tails(s, tail_ref[: n * TAIL, :], n, 1)
    for field, ref in ((cluster, query_cluster_ref), (rank, query_rank_ref)):
        columns = field.T
        for b in range(n):
            ref[b * s.base : (b + 1) * s.base, :] = jnp.broadcast_to(
                columns[: s.base, b : b + 1], (s.base, LANES)
            )
        if s.extra:
            at = n * s.base
            ref[at : at + n, :] = jnp.broadcast_to(field[:n, s.base : s.base + 1], (n, LANES))
            if s.query_rows > at + n:
                ref[at + n :, :] = jnp.zeros((s.query_rows - at - n, LANES), jnp.float32)
    if s.extra:
        at = n * s.base
        for c, piece in enumerate(pieces):
            spare = s.query_rows - at - piece.shape[0]
            if spare:
                piece = jnp.concatenate([piece, jnp.zeros((spare, LANES), jnp.float32)], axis=0)
            rows_ref[at:, c * LANES : (c + 1) * LANES] = piece.astype(jnp.bfloat16)


def match_keys(s, blocks, keys_ref, tail_ref, queries_ref, query_cluster_ref, query_rank_ref, best):
    n = len(blocks)
    group = s.per_lane_tile
    unpack(s, blocks, keys_ref, tail_ref)
    pieces, cluster, rank, padded = sorted_tails(s, tail_ref[: n * TAIL, :], n, group)
    key_cluster = key_lines(s, cluster, padded, group)
    key_rank = key_lines(s, rank, padded, group)
    queries = queries_ref[...]
    query_cluster = query_cluster_ref[...]
    query_rank = query_rank_ref[...]

    def take(best, scores, line_cluster, line_rank):
        usable = (query_cluster == line_cluster) & (line_rank < query_rank)
        return jnp.maximum(best, jnp.where(usable, scores, -1.0))

    tiles = n // group
    for first in range(0, tiles, 2):
        count = min(2, tiles - first)
        keys = keys_ref[first * LANES : (first + count) * LANES, :]
        scores = dot(queries, keys, ((1,), (1,)))
        for i in range(count):
            t = first + i
            best = take(
                best, scores[:, i * LANES : (i + 1) * LANES], key_cluster[t : t + 1], key_rank[t : t + 1]
            )
    if s.extra:
        count = group * padded
        spare = LANES - count
        for c, piece in enumerate(pieces):
            padded_piece = jnp.concatenate([piece, jnp.zeros((spare, LANES), jnp.float32)], axis=0) if spare else piece
            keys_ref[tiles * LANES :, c * LANES : (c + 1) * LANES] = padded_piece.astype(jnp.bfloat16)
        scores = dot(queries, keys_ref[tiles * LANES :, :], ((1,), (1,)))
        lines = []
        for field in (cluster, rank):
            line = field.T[s.base : s.base + 1, :]
            lines.append(jnp.concatenate([line, jnp.zeros((1, spare), jnp.float32)], axis=1) if spare else line)
        best = take(best, scores, *lines)
    return best


def write_best(s, order, best, out_ref):
    n = s.classes
    column = jnp.max(best, axis=1, keepdims=True)
    eye = iota((s.base, LANES), 0) == iota((s.base, LANES), 1)
    lane = iota((1, LANES), 1)
    me = my_class(s)
    for b, r in enumerate(order):
        line = jnp.sum(jnp.where(eye, column[b * s.base : (b + 1) * s.base], 0.0), axis=0, keepdims=True)
        if s.extra:
            at = n * s.base + b
            line = jnp.where(lane == s.base, column[at : at + 1], line)
        out_ref[pl.ds(me ^ r, 1), :, :] = line[None]


def first_kernel(s, order, query_count, key_count, last, *refs):
    refs = list(refs)
    query_blocks = blocks_of(refs[:query_count])
    key_refs = refs[query_count : query_count + key_count]
    outs = refs[query_count + key_count :]
    queries_ref, query_cluster_ref, query_rank_ref, best_ref, query_tail, keys_ref, key_tail = outs
    load_queries(s, query_blocks, queries_ref, query_tail, query_cluster_ref, query_rank_ref)
    best = jnp.full((s.query_rows, LANES), -1.0, jnp.float32)
    best = match_keys(
        s, query_blocks + blocks_of(key_refs), keys_ref, key_tail, queries_ref, query_cluster_ref, query_rank_ref, best
    )
    if last:
        write_best(s, order, best, best_ref)
    else:
        best_ref[...] = best


def next_kernel(s, order, key_count, last, *refs):
    queries_ref, query_cluster_ref, query_rank_ref, best_ref = refs[:4]
    key_refs = refs[4 : 4 + key_count]
    out_ref, keys_ref, key_tail = refs[4 + key_count :]
    best = match_keys(
        s, blocks_of(key_refs), keys_ref, key_tail, queries_ref, query_cluster_ref, query_rank_ref, best_ref[...]
    )
    if last:
        write_best(s, order, best, out_ref)
    else:
        out_ref[...] = best


def key_scratch(s, blocks):
    rows = blocks * s.base + (LANES if s.extra else 0)
    return [pltpu.VMEM((rows, s.width), jnp.bfloat16), pltpu.VMEM((blocks * TAIL, LANES), jnp.bfloat16)]


def cost(s, blocks):
    keys = blocks * s.base
    return pl.CostEstimate(
        flops=2 * s.query_rows * keys * s.width,
        transcendentals=0,
        bytes_accessed=2 * blocks * s.block_rows * LANES,
    )


def match_first(s, order, queries, keys, last):
    blocks = sum(a.shape[0] for a in queries + keys)
    best_shape = (s.classes, 1, LANES) if last else (s.query_rows, LANES)
    return pl.pallas_call(
        functools.partial(first_kernel, s, order, len(queries), len(keys), last),
        out_shape=[
            jax.ShapeDtypeStruct((s.query_rows, s.width), jnp.bfloat16),
            jax.ShapeDtypeStruct((s.query_rows, LANES), jnp.float32),
            jax.ShapeDtypeStruct((s.query_rows, LANES), jnp.float32),
            jax.ShapeDtypeStruct(best_shape, jnp.float32),
        ],
        scratch_shapes=[pltpu.VMEM((s.classes * TAIL, LANES), jnp.bfloat16)] + key_scratch(s, blocks),
        compiler_params=pltpu.CompilerParams(vmem_limit_bytes=VMEM_LIMIT),
        cost_estimate=cost(s, blocks),
        name="match_first",
    )(*queries, *keys)


def match_next(s, order, state, keys, last):
    blocks = sum(a.shape[0] for a in keys)
    best_shape = (s.classes, 1, LANES) if last else (s.query_rows, LANES)
    best = pl.pallas_call(
        functools.partial(next_kernel, s, order, len(keys), last),
        out_shape=jax.ShapeDtypeStruct(best_shape, jnp.float32),
        scratch_shapes=key_scratch(s, blocks),
        compiler_params=pltpu.CompilerParams(vmem_limit_bytes=VMEM_LIMIT),
        cost_estimate=cost(s, blocks),
        name="match_next",
    )(*state, *keys)
    return [*state[:3], best]


def collect_kernel(s, info_ref, best_ref, out_ref):
    n = s.classes
    best = best_ref[...].reshape(n, LANES)
    parts = []
    for _ in range(3):
        part = best.astype(jnp.bfloat16)
        parts.append(part.astype(jnp.float32))
        best = best - parts[-1]
    target = info_ref[0:1, :]
    within = info_ref[1:2, :]
    pick = (iota((LANES, s.rows), 0) == within).astype(jnp.float32).astype(jnp.bfloat16)
    found = dot(jnp.concatenate(parts, axis=0).astype(jnp.bfloat16), pick)
    found = found[:n] + found[n : 2 * n] + found[2 * n :]
    mine = iota((n, s.rows), 0) == target
    line = jnp.sum(jnp.where(mine, found, 0.0), axis=0, keepdims=True)
    for i in range(s.rows // LANES):
        out_ref[i : i + 1, :] = line[:, i * LANES : (i + 1) * LANES]


def collect(s, info, best):
    out = pl.pallas_call(
        functools.partial(collect_kernel, s),
        out_shape=jax.ShapeDtypeStruct((s.rows // LANES, LANES), jnp.float32),
        compiler_params=pltpu.CompilerParams(vmem_limit_bytes=8 * 1024 * 1024),
        name="collect",
    )(info, best)
    return out.reshape(s.rows)


def swap(array, axis, flip):
    size = lax.axis_size(axis)
    return lax.ppermute(array, axis, [(i, i ^ flip) for i in range(size)])


def local(embed, cluster, rank):
    s = Shape(embed.shape[0], embed.shape[1], lax.axis_size("z"), lax.axis_size("x"), lax.axis_size("y"))
    order = [s.x * k + j for k in range(s.z) for j in range(s.x)]
    info, *blocks = place(s, [[s.x * k + j for j in range(s.x)] for k in range(s.z)], embed, cluster, rank)
    arrived = {k: swap(blocks[k], "z", k) if k else blocks[k] for k in reversed(range(s.z))}
    near = swap(jnp.concatenate([arrived[0][1:], arrived[1][1:]]), "x", 1)
    queries = [jnp.concatenate([arrived[0][:1], near[:1], arrived[1][:1], near[1:]])]
    queries += [jnp.concatenate([arrived[k][:1], swap(arrived[k][1:], "x", 1)]) for k in range(2, s.z)]
    state = match_first(s, order, queries, [], False)
    if s.y == 2:
        waves = []
        for a in queries:
            over = swap(a, "y", 1)
            waves.append([over, swap(jnp.concatenate([a, over]), "core", 1)])
        state = match_next(s, order, state, [wave[0] for wave in waves] + [waves[0][1]], False)
        state = match_next(s, order, state, [wave[1] for wave in waves[1:]], True)
    else:
        everyone = lax.all_gather(jnp.concatenate(queries), ("core", "y"), axis=0)
        me = lax.axis_index(("core", "y"))
        size = everyone.shape[0]
        for i in range(1, size):
            keys = lax.dynamic_index_in_dim(everyone, (me + i) % size, keepdims=False)
            state = match_next(s, order, state, [keys], i == size - 1)
    returned = lax.all_to_all(state[3], ("z", "x"), split_axis=0, concat_axis=0, tiled=True)
    return collect(s, info, returned)


def solution(mesh):
    store, own = mesh.shape["store"], mesh.shape["own"]
    split = Mesh(mesh.devices.reshape(store // 2, 2, own // 2, 2), ("z", "core", "y", "x"))
    spread = ("z", "core", "y", "x")
    return jax.shard_map(
        local,
        mesh=split,
        in_specs=(P(spread, None), P(spread), P(spread)),
        out_specs=P(spread),
        check_vma=False,
    )
```
